512 devices in a mesh: sub: 8 (over y), row: 8 (over z), col: 8 (over x, core).
Axes of the slice: x: 4, y: 8, z: 8, core: 2. Of those that a mesh axis runs over, the one named last changes fastest.
Arguments:
- front: float32 [12288, 12288], P(('sub', 'row'), 'col'), as said below
- child_tiles: float32 [32768, 4096], P(('sub', 'row', 'col')), may hold values from -1.5 to 1.5
- child_target: int32 [32768], P(('sub', 'row', 'col')), may hold values from 0 to 36863, as said below
- child_rows: int32 [32768], P(('sub', 'row', 'col')), may hold values from 1 to 64
- child_cols: int32 [32768], P(('sub', 'row', 'col')), may hold values from 1 to 64
Outputs:
- factored: float32 [12288, 12288], P(('sub', 'row'), 'col')
The draws below stay inside these ranges and needn't reach their ends.
Inputs may be any that keep to these rules, and one draw needn't show every extreme that they name: `child_target`: tile k held by a device of col index c targets a tile column within that device's columns, c * (24) and on; the tiles of one device go to at most 2 tiles of any one owner along sub+row, and some owner receives 2 from every device. The front is symmetric and positive definite.
All inputs are finite; a program needn't handle non-finite values.
Results may differ from the reference program's by a relative error of at most 0.0003.
Values sent between devices are 32-bit elements; how exact they have to be, the bound alone decides.
No kernel may reach another device: no remote copies, remote signals or barrier semaphores. Data moves between devices by JAX's collectives and lax.ppermute only.
A program may use at most 64 MiB of HBM per device.

```python
import jax
import jax.numpy as jnp
from jax import lax

FRONT = 12288
TILE = 64
PANEL = 192
STEPS = 3
CHILD_DEV = 64
CAP = 2
CHILDREN = 32768
N_SUB = 8
N_ROW = 8
N_COL = 8


def laplace_front(points, reach, height, shift):
    dist_sq = jnp.zeros((FRONT, FRONT), jnp.float32)
    for axis_pos in range(3):
        coord = points[:, axis_pos]
        gap = coord[:, None] - coord[None, :]
        dist_sq = dist_sq + gap * gap
    kernel = height * jnp.exp(-jnp.sqrt(dist_sq) / reach)
    return kernel + jnp.diag(shift)


def draw_front(key, part):
    key = jax.random.fold_in(key, 5)
    points = jax.random.uniform(jax.random.fold_in(key, 1), (FRONT, 3), jnp.float32, 0.0, 1.0)
    shift = jax.random.uniform(jax.random.fold_in(key, 2), (FRONT,), jnp.float32, 16.0, 32.0)
    return laplace_front(points, 2.0, 24.0, shift)


def draw_child_target(key, part):
    key = jax.random.fold_in(key, 11)
    wide_count = N_SUB * N_ROW
    slot_count = wide_count * CAP
    device_count = N_SUB * N_ROW * N_COL
    tiles_down = FRONT // wide_count // TILE
    tiles_across = FRONT // N_COL // TILE
    favored = jax.random.randint(jax.random.fold_in(key, 1), (), 0, wide_count)

    def per_device(device):
        dev_key = jax.random.fold_in(key, device + 2)
        shuffled = jax.random.permutation(jax.random.fold_in(dev_key, 0), slot_count)
        priority = jnp.where(shuffled // CAP == favored, 0, 1).astype(jnp.int32)
        chosen = shuffled[jnp.argsort(priority, stable=True)][:CHILD_DEV]
        target_dev = chosen // CAP
        col_pos = device % N_COL
        tile_row = target_dev * tiles_down + jax.random.randint(jax.random.fold_in(dev_key, 1), (CHILD_DEV,), 0, tiles_down)
        tile_col = col_pos * tiles_across + jax.random.randint(jax.random.fold_in(dev_key, 2), (CHILD_DEV,), 0, tiles_across)
        return (tile_row * (FRONT // TILE) + tile_col).astype(jnp.int32)
    return jax.vmap(per_device)(jnp.arange(device_count, dtype=jnp.int32)).reshape(-1)


def plant(entries, rng, low, top_value):
    spot = [jax.random.randint(jax.random.fold_in(rng, axis), (), 0, length) for axis, length in enumerate(entries.shape)]
    widest = entries.shape.index(max(entries.shape))
    next_to = spot[:widest] + [(spot[widest] + 1) % entries.shape[widest]] + spot[widest + 1:]
    return entries.at[tuple(spot)].set(low).at[tuple(next_to)].set(top_value)


def levels(key, shape, split, low, largest):
    def one(position, shards_of):
        heights = jax.random.uniform(jax.random.fold_in(jax.random.fold_in(key, 6), position), (shards_of,), jnp.float32, low / len(split), largest / len(split))
        return jnp.repeat(jnp.exp(heights), shape[position] // shards_of).reshape((-1,) + (1,) * (len(shape) - position - 1))

    factor_of = one(*split[0])
    for cut in split[1:]:
        factor_of = factor_of * one(*cut)
    return factor_of


def scatter_about(own_key, extent, scale, most, split=(), kind=jnp.bfloat16):
    values = scale * jax.random.normal(own_key, extent, jnp.float32)
    if split:
        values = values * levels(own_key, extent, split, -0.22, 0.18)
    return jnp.clip(values, -most, most).astype(kind)


def setup_inputs(seed: int = 0) -> dict:
    keys = jax.random.split(jax.random.key(seed), 6)
    return {
        "front": draw_front(jax.random.fold_in(keys[5], 71), 0),
        "child_tiles": scatter_about(keys[1], (CHILDREN, TILE * TILE), 0.25, 1.5, ((0, 512),), jnp.float32),
        "child_target": draw_child_target(jax.random.fold_in(keys[5], 71), 0),
        "child_rows": plant(jax.random.randint(keys[3], (CHILDREN,), 1, TILE + 1), jax.random.fold_in(keys[3], 1), 1, TILE).astype(jnp.int32),
        "child_cols": plant(jax.random.randint(keys[4], (CHILDREN,), 1, TILE + 1), jax.random.fold_in(keys[4], 1), 1, TILE).astype(jnp.int32),
    }


def reference(front, child_tiles, child_target, child_rows, child_cols):
    order_tiles = FRONT // TILE
    lane_index = jnp.arange(TILE * TILE, dtype=jnp.int32)
    within = ((lane_index // TILE)[None, :] < child_rows[:, None]) & ((lane_index % TILE)[None, :] < child_cols[:, None])
    masked = jnp.where(within, child_tiles, jnp.float32(0.0)).reshape(-1, TILE, TILE)
    tiled_front = front.reshape(order_tiles, TILE, order_tiles, TILE)
    tile_row = (child_target // order_tiles).astype(jnp.int32)
    tile_col = (child_target % order_tiles).astype(jnp.int32)
    tiled_front = tiled_front.at[tile_row, :, tile_col, :].add(masked)
    matrix = tiled_front.reshape(FRONT, FRONT)
    cols_all = jnp.arange(FRONT, dtype=jnp.int32)
    for panel_step in range(STEPS):
        first_col = panel_step * PANEL
        last_col = first_col + PANEL
        factor = jnp.linalg.cholesky(matrix[first_col:last_col, first_col:last_col])
        solved = lax.linalg.triangular_solve(factor, matrix[first_col:last_col, :], left_side=True, lower=True)
        solved = jnp.where(cols_all[None, :] >= first_col, solved, jnp.float32(0.0))
        trailing = solved[:, last_col:]
        update = jnp.dot(trailing.T.astype(jnp.float32), trailing.astype(jnp.float32), precision=lax.Precision.HIGHEST, preferred_element_type=jnp.float32)
        matrix = matrix.at[last_col:, last_col:].set(matrix[last_col:, last_col:] - update)
        matrix = matrix.at[first_col:last_col, :].set(solved)
    return matrix
```

```python
import functools

import jax
import jax.numpy as jnp
from jax import lax
from jax.experimental import pallas as pl
from jax.experimental.pallas import tpu as pltpu
from jax.sharding import PartitionSpec as P

FRONT = 12288
TILE = 64
PANEL = 192
STEPS = 3
TOP = PANEL * STEPS
WIDE = 64
CAP = 2
SLOTS = WIDE * CAP
TOP_SLOTS = STEPS * CAP
HALF_ROWS = TILE // 2
HIGHEST = lax.Precision.HIGHEST
MIB = 1024 * 1024


def vmem():
    return pl.BlockSpec(memory_space=pltpu.VMEM)


def smem():
    return pl.BlockSpec(memory_space=pltpu.SMEM)


def dot(a, b, dims):
    return lax.dot_general(a, b, (dims, ((), ())), precision=HIGHEST, preferred_element_type=jnp.float32)


def split_halves(first, second):
    low = lax.broadcasted_iota(jnp.int32, first.shape, 1) < TILE
    even = jnp.where(low, first, pltpu.roll(second, TILE, 1))
    odd = jnp.where(low, pltpu.roll(first, TILE, 1), second)
    return even, odd


def sort_kernel(owner, place, rows, cols, tiles, slots, top_rows, slot_place, top_buf, count):
    def clear(i, _):
        count[i] = 0
        slot_place[2 * i] = -1
        slot_place[2 * i + 1] = -1
        return 0

    lax.fori_loop(0, WIDE, clear, 0)
    top_buf[...] = jnp.zeros_like(top_buf)
    line = lax.broadcasted_iota(jnp.int32, (HALF_ROWS, 128), 0)
    lane = lax.broadcasted_iota(jnp.int32, (HALF_ROWS, 128), 1)
    tile_row = 2 * line + lane // TILE
    tile_col = lane % TILE

    def one(k, _):
        to = owner[k]
        rank = jnp.minimum(count[to], CAP - 1)
        count[to] = rank + 1
        slot = CAP * to + rank
        slot_place[slot] = place[k]
        inside = (tile_row < rows[k]) & (tile_col < cols[k])
        kept = jnp.where(inside, tiles[k], 0.0)
        slots[slot] = kept

        @pl.when(to < STEPS)
        def _():
            top_buf[slot] = kept

        return 0

    lax.fori_loop(0, tiles.shape[0], one, 0)
    for q in range(STEPS):
        even, odd = split_halves(top_buf[2 * q], top_buf[2 * q + 1])
        top_rows[q, pl.ds(0, HALF_ROWS, stride=2), :] = even
        top_rows[q, pl.ds(1, HALF_ROWS, stride=2), :] = odd


def sort_tiles(owner, place, rows, cols, tiles):
    return pl.pallas_call(
        sort_kernel,
        out_shape=(
            jax.ShapeDtypeStruct((SLOTS, HALF_ROWS, 128), jnp.float32),
            jax.ShapeDtypeStruct((STEPS, TILE, 128), jnp.float32),
            jax.ShapeDtypeStruct((SLOTS,), jnp.int32),
        ),
        in_specs=[smem()] * 4 + [vmem()],
        out_specs=(vmem(), vmem(), smem()),
        scratch_shapes=[
            pltpu.VMEM((TOP_SLOTS, HALF_ROWS, 128), jnp.float32),
            pltpu.SMEM((WIDE,), jnp.int32),
        ],
        compiler_params=pltpu.CompilerParams(vmem_limit_bytes=24 * MIB),
        cost_estimate=pl.CostEstimate(flops=1_000_000, bytes_accessed=3_200_000, transcendentals=0),
        name="sort_tiles",
    )(owner, place, rows, cols, tiles)


def extend_kernel(place, tiles, front, out, total, stage):
    down, across = front.shape[0] // TILE, front.shape[1] // TILE
    total[...] = jnp.zeros_like(total)

    def one(n, _):
        at = place[n]
        at = jnp.where(at < 0, down * across, at)
        total[at] = total[at] + tiles[n]
        return 0

    lax.fori_loop(0, tiles.shape[0], one, 0)
    for r in range(down):
        for pair in range(across // 2):
            at = r * across + 2 * pair
            even, odd = split_halves(total[at], total[at + 1])
            stage[at // 2, pl.ds(0, HALF_ROWS, stride=2), :] = even
            stage[at // 2, pl.ds(1, HALF_ROWS, stride=2), :] = odd
            spot = (slice(TILE * r, TILE * r + TILE), slice(128 * pair, 128 * pair + 128))
            out[spot] = front[spot] + stage[at // 2]


def extend(place, tiles, front):
    count = (front.shape[0] // TILE) * (front.shape[1] // TILE)
    return pl.pallas_call(
        extend_kernel,
        out_shape=jax.ShapeDtypeStruct(front.shape, jnp.float32),
        in_specs=[smem(), vmem(), vmem()],
        out_specs=vmem(),
        scratch_shapes=[
            pltpu.VMEM((count + 1, HALF_ROWS, 128), jnp.float32),
            pltpu.VMEM((count // 2, TILE, 128), jnp.float32),
        ],
        compiler_params=pltpu.CompilerParams(vmem_limit_bytes=24 * MIB),
        cost_estimate=pl.CostEstimate(flops=1_000_000, bytes_accessed=4_500_000, transcendentals=0),
        name="extend",
    )(place, tiles, front)


def lanes_of(group, col):
    return jnp.broadcast_to(group[:, col : col + 1], (8, 128))


def row_of(group, row):
    return jnp.broadcast_to(group[row : row + 1, :], (8, 128))


def eliminate_block(block):
    sub = lax.broadcasted_iota(jnp.int32, (8, 128), 0)
    for g in range(8):
        spread = [lanes_of(block[g], 8 * g + i) for i in range(8)]
        pivot = {(m, n): row_of(spread[n], m) for m in range(8) for n in range(m, 8)}
        low = {}
        inv = [None] * 8
        for i in range(0, 8, 2):
            a, b, c = pivot[i, i], pivot[i, i + 1], pivot[i + 1, i + 1]
            inv[i] = lax.rsqrt(a)
            inv[i + 1] = (a * inv[i]) * lax.rsqrt(a * c - b * b)
            low[i + 1, i] = b * inv[i]
            for m in range(i + 2, 8):
                low[m, i] = pivot[i, m] * inv[i]
                low[m, i + 1] = (pivot[i + 1, m] - low[m, i] * low[i + 1, i]) * inv[i + 1]
            for m in range(i + 2, 8):
                for n in range(m, 8):
                    pivot[m, n] = pivot[m, n] - low[m, i] * low[n, i] - low[m, i + 1] * low[n, i + 1]
        out = []
        for m in range(8):
            row = row_of(block[g], m)
            for t in range(m):
                row = row - low[m, t] * out[t]
            out.append(row * inv[m])
        for q in range(g + 1, 8):
            left = []
            reduced = block[q]
            for i in range(8):
                col = lanes_of(block[q], 8 * g + i)
                for t in range(i):
                    col = col - left[t] * low[i, t]
                left.append(col * inv[i])
            for i in range(8):
                reduced = reduced - left[i] * out[i]
            block[q] = reduced
        rows = out[0]
        for m in range(1, 8):
            rows = jnp.where(sub == m, out[m], rows)
        block[g] = rows
    return block


def factor_kernel(corner, work):
    work[...] = corner[...]
    sub = lax.broadcasted_iota(jnp.int32, (TILE, 128), 0)
    lane = lax.broadcasted_iota(jnp.int32, (TILE, 128), 1)
    right_eye = jnp.where(lane == sub + TILE, 1.0, 0.0)
    for k in range(TOP // TILE):
        o = TILE * k
        start = 128 * (o // 128)
        block = work[o : o + TILE, start : min(start + 128, TOP)]
        if start + 128 > TOP:
            block = jnp.concatenate([block, jnp.zeros((TILE, TILE), jnp.float32)], axis=1)
        if o != start:
            block = pltpu.roll(block, TILE, 1)
        block = jnp.where(lane < TILE, block, right_eye)
        groups = eliminate_block([block[8 * q : 8 * q + 8, :] for q in range(8)])
        block = jnp.concatenate(groups, axis=0)
        part = pltpu.roll(block, TILE, 1)[:, :TILE]
        row = lax.broadcasted_iota(jnp.int32, (TILE, TOP), 0)
        col = lax.broadcasted_iota(jnp.int32, (TILE, TOP), 1) - o
        own = (col >= 0) & (col < TILE)
        slab = dot(part, jnp.where(own, jnp.where(col == row, 1.0, 0.0), work[o : o + TILE, :]), ((1,), (0,)))
        work[o : o + TILE, :] = slab
        for top, bottom in ((o + TILE, o + 2 * TILE), (o + 2 * TILE, TOP)):
            if top >= TOP or top == bottom:
                continue
            update = dot(slab[:, top:bottom], slab, ((0,), (0,)))
            col = lax.broadcasted_iota(jnp.int32, (bottom - top, TOP), 1) - o
            own = (col >= 0) & (col < TILE)
            work[top:bottom, :] = jnp.where(own, 0.0, work[top:bottom, :]) - update


def factor_corner(corner):
    return pl.pallas_call(
        factor_kernel,
        out_shape=jax.ShapeDtypeStruct((TOP, TOP), jnp.float32),
        in_specs=[vmem()],
        out_specs=vmem(),
        compiler_params=pltpu.CompilerParams(vmem_limit_bytes=24 * MIB),
        cost_estimate=pl.CostEstimate(flops=25_000_000_000, bytes_accessed=2_700_000, transcendentals=1000),
        name="factor_corner",
    )(corner)


def panel_order():
    row = lax.broadcasted_iota(jnp.int32, (TOP, TOP), 0)
    col = lax.broadcasted_iota(jnp.int32, (TOP, TOP), 1)
    source = jnp.where(row < 8 * WIDE, (row % 8) * WIDE + row // 8, row)
    return jnp.where(col == source, 1.0, 0.0)


def weights_kernel(flags, side, corner, weights, solved):
    row = lax.broadcasted_iota(jnp.int32, (TOP, TOP), 0) // TILE
    col = lax.broadcasted_iota(jnp.int32, (TOP, TOP), 1) // TILE
    inverse = jnp.where(row >= col, corner[...], 0.0)
    solved[...] = dot(inverse, side[...], ((1,), (0,)))
    order = panel_order()

    @pl.when(flags[2] == 0)
    def _():
        weights[...] = dot(order, dot(inverse, solved[...], ((0,), (0,))), ((1,), (0,)))

    @pl.when(flags[2] == 1)
    def _():
        first = pl.multiple_of(flags[3] * PANEL, PANEL)
        row = (lax.broadcasted_iota(jnp.int32, (PANEL, TOP), 0) + first) // TILE
        col = lax.broadcasted_iota(jnp.int32, (PANEL, TOP), 1) // TILE
        own = jnp.where(row >= col, corner[pl.ds(first, PANEL), :], 0.0)
        weights[...] = -dot(order, own, ((1,), (1,)))


def make_weights(flags, side, corner):
    shape = jax.ShapeDtypeStruct((TOP, PANEL), jnp.float32)
    return pl.pallas_call(
        weights_kernel,
        out_shape=(shape, shape),
        in_specs=[smem(), vmem(), vmem()],
        out_specs=(vmem(), vmem()),
        compiler_params=pltpu.CompilerParams(vmem_limit_bytes=24 * MIB),
        cost_estimate=pl.CostEstimate(flops=3_000_000_000, bytes_accessed=2_500_000, transcendentals=0),
        name="make_weights",
    )(flags, side, corner)


def finish_kernel(flags, weights, side, corner, panel, base, out):
    lines = base.shape[1] // 128
    for pair in range(lines // 2):
        cols = []
        for line in (2 * pair, 2 * pair + 1):
            block = panel[:, 8 * line : 8 * line + 8, :].reshape(8 * WIDE, 128)
            last = panel[:, 8 * lines + line, :]
            cols.append(jnp.concatenate([block, last], axis=0))
        update = dot(weights[...], jnp.concatenate(cols, axis=1), ((0,), (0,)))
        first = 256 * pair
        spot = slice(first, first + 256)
        col = lax.broadcasted_iota(jnp.int32, update.shape, 1) + first
        kept = jnp.where(flags[2] == 1, 0.0, base[:, spot])
        out[:, spot] = jnp.where(col < flags[0], 0.0, kept - update)

    @pl.when(flags[1] == 1)
    def _():
        row = lax.broadcasted_iota(jnp.int32, (TOP, TOP), 0) // PANEL
        col = lax.broadcasted_iota(jnp.int32, (TOP, TOP), 1) // PANEL
        strict = jnp.where(row < col, corner[...], 0.0)
        out[:, :TOP] = base[:, :TOP] - dot(side[...], strict, ((0,), (0,)))


def finish(flags, weights, side, corner, panel, base):
    return pl.pallas_call(
        finish_kernel,
        out_shape=jax.ShapeDtypeStruct(base.shape, jnp.float32),
        in_specs=[smem()] + [vmem()] * 5,
        out_specs=vmem(),
        compiler_params=pltpu.CompilerParams(vmem_limit_bytes=32 * MIB),
        cost_estimate=pl.CostEstimate(flops=2_500_000_000, bytes_accessed=9_000_000, transcendentals=0),
        name="finish",
    )(flags, weights, side, corner, panel, base)


def exchange(values, axes):
    return lax.all_to_all(values, axes, split_axis=0, concat_axis=0, tiled=True)


def local(front, child_tiles, child_target, child_rows, child_cols):
    my_row = lax.axis_index("row")
    my_sub = lax.axis_index("sub")
    my_col = lax.axis_index("col")
    my_block = my_sub * 8 + my_row
    block_rows, block_cols = front.shape
    order_tiles = FRONT // TILE
    tiles_down = block_rows // TILE
    tiles_across = block_cols // TILE
    here = tiles_down * tiles_across
    tile_row = child_target // order_tiles
    tile_col = child_target % order_tiles
    owner = tile_row // tiles_down
    place = (tile_row - owner * tiles_down) * tiles_across + tile_col - my_col * tiles_across
    slots, top_rows, slot_place = sort_tiles(
        owner, place, child_rows, child_cols, child_tiles.reshape(-1, HALF_ROWS, 128)
    )

    top_place = slot_place[:TOP_SLOTS]
    top_place = jnp.where(top_place < 0, -1, top_place + here * (jnp.arange(TOP_SLOTS) // CAP))
    meta = jnp.concatenate(
        [
            jnp.broadcast_to(top_place[None, :], (WIDE, TOP_SLOTS)),
            slot_place.reshape(WIDE, CAP),
            jnp.zeros((WIDE, 128 - TOP_SLOTS - CAP), jnp.int32),
        ],
        axis=1,
    ).astype(jnp.float32)
    front_rows = front.reshape(tiles_down, TILE, block_cols // 128, 128).transpose(1, 0, 2, 3)
    sent = jnp.concatenate(
        [top_rows.transpose(1, 0, 2), meta[:, None, :], front_rows.reshape(TILE, -1, 128)], axis=1
    )
    got = exchange(sent, ("sub", "row"))
    got_meta = got[:, STEPS, :].astype(jnp.int32)
    in_place = got_meta[:, TOP_SLOTS : TOP_SLOTS + CAP].reshape(-1)
    in_top = got_meta[:, :TOP_SLOTS].reshape(-1)
    pieces = got[:, :STEPS, :].reshape(-1, TILE)
    one_hot = (jnp.arange(STEPS * here, dtype=jnp.int32)[:, None] == in_top[None, :]).astype(jnp.float32)
    held = dot(one_hot, pieces, ((1,), (0,))).reshape(STEPS * tiles_down, block_cols)
    held = held + got[:STEPS, STEPS + 1 :, :].reshape(STEPS * tiles_down, block_cols)

    lines = block_cols // 128
    whole = held[:8].reshape(8, lines, 128).transpose(1, 0, 2).reshape(8 * lines, 128)
    panel = lax.all_gather(
        jnp.concatenate([whole, held[8].reshape(lines, 128)], axis=0), ("sub", "row"), axis=0, tiled=False
    )

    part_cols = PANEL // 8
    side_size = 9 * part_cols
    packed = jnp.concatenate([held[0:3, :TOP], held[3:6, PANEL:TOP], held[6:9, 2 * PANEL : TOP]], axis=1)
    corner_cols = packed.shape[1] // 8
    corner_send = packed.reshape(3, 8, corner_cols).transpose(1, 0, 2).reshape(8, -1)
    side_send = held.reshape(9, 8, 8, part_cols).transpose(2, 1, 0, 3).reshape(8, -1)
    got = exchange(jnp.concatenate([side_send, corner_send], axis=1), "col")
    side_send = got[:, : 8 * side_size].reshape(WIDE, side_size)
    corner_send = jnp.broadcast_to(got[0:1, 8 * side_size :], (WIDE, 3 * corner_cols))
    got = exchange(jnp.concatenate([side_send, corner_send], axis=1), ("sub", "row"))
    got, slots = lax.optimization_barrier((got, slots))
    arrived = exchange(slots.reshape(WIDE, CAP * HALF_ROWS, 128), ("sub", "row")).reshape(SLOTS, HALF_ROWS, 128)
    got = exchange(jnp.broadcast_to(got[None], (8,) + got.shape), "col")
    side = got[:, :, :side_size].reshape(8, WIDE, 9, part_cols).transpose(2, 1, 0, 3).reshape(TOP, PANEL)
    packed = got[:, :, side_size:].reshape(8, WIDE, 3, corner_cols).transpose(2, 1, 0, 3).reshape(PANEL, -1)

    def balanced(square):
        return 0.5 * (square + square.T)

    def blank(cols):
        return jnp.zeros((PANEL, cols), jnp.float32)

    second = packed[:, TOP : TOP + 2 * PANEL]
    corner = jnp.concatenate(
        [
            jnp.concatenate([balanced(packed[:, :PANEL]), packed[:, PANEL:TOP]], axis=1),
            jnp.concatenate([blank(PANEL), balanced(second[:, :PANEL]), second[:, PANEL:]], axis=1),
            jnp.concatenate([blank(2 * PANEL), balanced(packed[:, TOP + 2 * PANEL :])], axis=1),
        ],
        axis=0,
    )
    corner = factor_corner(corner)

    is_owner = my_block < STEPS
    flags = jnp.stack(
        [
            jnp.where(is_owner, my_block * PANEL - my_col * block_cols, 0),
            ((my_col == 0) & ~is_owner).astype(jnp.int32),
            is_owner.astype(jnp.int32),
            jnp.minimum(my_block, STEPS - 1),
        ]
    ).astype(jnp.int32)
    weights, solved_side = make_weights(flags, side, corner)
    matrix = extend(in_place, arrived, front)
    return finish(flags, weights, solved_side, corner, panel, matrix)


def solution(mesh):
    in_specs = (
        P(("sub", "row"), "col"),
        P(("sub", "row", "col"), None),
        P(("sub", "row", "col")),
        P(("sub", "row", "col")),
        P(("sub", "row", "col")),
    )
    out_specs = P(("sub", "row"), "col")
    return jax.shard_map(local, mesh=mesh, in_specs=in_specs, out_specs=out_specs, check_vma=False)
```

```python
import functools

import jax
import jax.numpy as jnp
from jax import lax
from jax.experimental import pallas as pl
from jax.experimental.pallas import tpu as pltpu
from jax.sharding import PartitionSpec as P

FRONT = 12288
TILE = 64
PANEL = 192
STEPS = 3
TOP = PANEL * STEPS
WIDE = 64
CAP = 2
SLOTS = WIDE * CAP
TOP_SLOTS = STEPS * CAP
HALF_ROWS = TILE // 2
HIGHEST = lax.Precision.HIGHEST
MIB = 1024 * 1024


def vmem():
    return pl.BlockSpec(memory_space=pltpu.VMEM)


def smem():
    return pl.BlockSpec(memory_space=pltpu.SMEM)


def dot(a, b, dims):
    return lax.dot_general(a, b, (dims, ((), ())), precision=HIGHEST, preferred_element_type=jnp.float32)


def split_halves(first, second):
    low = lax.broadcasted_iota(jnp.int32, first.shape, 1) < TILE
    even = jnp.where(low, first, pltpu.roll(second, TILE, 1))
    odd = jnp.where(low, pltpu.roll(first, TILE, 1), second)
    return even, odd


def sort_kernel(owner, place, rows, cols, tiles, slots, top_rows, slot_place, top_buf, count):
    def clear(i, _):
        count[i] = 0
        slot_place[2 * i] = -1
        slot_place[2 * i + 1] = -1
        return 0

    lax.fori_loop(0, WIDE, clear, 0)
    top_buf[...] = jnp.zeros_like(top_buf)
    line = lax.broadcasted_iota(jnp.int32, (HALF_ROWS, 128), 0)
    lane = lax.broadcasted_iota(jnp.int32, (HALF_ROWS, 128), 1)
    tile_row = 2 * line + lane // TILE
    tile_col = lane % TILE

    def one(k, _):
        to = owner[k]
        rank = jnp.minimum(count[to], CAP - 1)
        count[to] = rank + 1
        slot = CAP * to + rank
        slot_place[slot] = place[k]
        inside = (tile_row < rows[k]) & (tile_col < cols[k])
        kept = jnp.where(inside, tiles[k], 0.0)
        slots[slot] = kept

        @pl.when(to < STEPS)
        def _():
            top_buf[slot] = kept

        return 0

    lax.fori_loop(0, tiles.shape[0], one, 0)
    for q in range(STEPS):
        even, odd = split_halves(top_buf[2 * q], top_buf[2 * q + 1])
        top_rows[q, pl.ds(0, HALF_ROWS, stride=2), :] = even
        top_rows[q, pl.ds(1, HALF_ROWS, stride=2), :] = odd


def sort_tiles(owner, place, rows, cols, tiles):
    return pl.pallas_call(
        sort_kernel,
        out_shape=(
            jax.ShapeDtypeStruct((SLOTS, HALF_ROWS, 128), jnp.float32),
            jax.ShapeDtypeStruct((STEPS, TILE, 128), jnp.float32),
            jax.ShapeDtypeStruct((SLOTS,), jnp.int32),
        ),
        in_specs=[smem()] * 4 + [vmem()],
        out_specs=(vmem(), vmem(), smem()),
        scratch_shapes=[
            pltpu.VMEM((TOP_SLOTS, HALF_ROWS, 128), jnp.float32),
            pltpu.SMEM((WIDE,), jnp.int32),
        ],
        compiler_params=pltpu.CompilerParams(vmem_limit_bytes=24 * MIB),
        cost_estimate=pl.CostEstimate(flops=1_000_000, bytes_accessed=3_200_000, transcendentals=0),
        name="sort_tiles",
    )(owner, place, rows, cols, tiles)


def extend_kernel(place, tiles, front, out, total, stage):
    down, across = front.shape[0] // TILE, front.shape[1] // TILE
    total[...] = jnp.zeros_like(total)

    def one(n, _):
        at = place[n]
        at = jnp.where(at < 0, down * across, at)
        total[at] = total[at] + tiles[n]
        return 0

    lax.fori_loop(0, tiles.shape[0], one, 0)
    for r in range(down):
        for pair in range(across // 2):
            at = r * across + 2 * pair
            even, odd = split_halves(total[at], total[at + 1])
            stage[at // 2, pl.ds(0, HALF_ROWS, stride=2), :] = even
            stage[at // 2, pl.ds(1, HALF_ROWS, stride=2), :] = odd
            spot = (slice(TILE * r, TILE * r + TILE), slice(128 * pair, 128 * pair + 128))
            out[spot] = front[spot] + stage[at // 2]


def extend(place, tiles, front):
    count = (front.shape[0] // TILE) * (front.shape[1] // TILE)
    return pl.pallas_call(
        extend_kernel,
        out_shape=jax.ShapeDtypeStruct(front.shape, jnp.float32),
        in_specs=[smem(), vmem(), vmem()],
        out_specs=vmem(),
        scratch_shapes=[
            pltpu.VMEM((count + 1, HALF_ROWS, 128), jnp.float32),
            pltpu.VMEM((count // 2, TILE, 128), jnp.float32),
        ],
        compiler_params=pltpu.CompilerParams(vmem_limit_bytes=24 * MIB),
        cost_estimate=pl.CostEstimate(flops=1_000_000, bytes_accessed=4_500_000, transcendentals=0),
        name="extend",
    )(place, tiles, front)


def lanes_of(group, col):
    return jnp.broadcast_to(group[:, col : col + 1], (8, 128))


def row_of(group, row):
    return jnp.broadcast_to(group[row : row + 1, :], (8, 128))


def eliminate_block(block):
    sub = lax.broadcasted_iota(jnp.int32, (8, 128), 0)
    for g in range(8):
        spread = [lanes_of(block[g], 8 * g + i) for i in range(8)]
        pivot = {(m, n): row_of(spread[n], m) for m in range(8) for n in range(m, 8)}
        low = {}
        inv = [None] * 8
        for i in range(0, 8, 2):
            a, b, c = pivot[i, i], pivot[i, i + 1], pivot[i + 1, i + 1]
            inv[i] = lax.rsqrt(a)
            inv[i + 1] = (a * inv[i]) * lax.rsqrt(a * c - b * b)
            low[i + 1, i] = b * inv[i]
            for m in range(i + 2, 8):
                low[m, i] = pivot[i, m] * inv[i]
                low[m, i + 1] = (pivot[i + 1, m] - low[m, i] * low[i + 1, i]) * inv[i + 1]
            for m in range(i + 2, 8):
                for n in range(m, 8):
                    pivot[m, n] = pivot[m, n] - low[m, i] * low[n, i] - low[m, i + 1] * low[n, i + 1]
        out = []
        for m in range(8):
            row = row_of(block[g], m)
            for t in range(m):
                row = row - low[m, t] * out[t]
            out.append(row * inv[m])
        for q in range(g + 1, 8):
            left = []
            reduced = block[q]
            for i in range(8):
                col = lanes_of(block[q], 8 * g + i)
                for t in range(i):
                    col = col - left[t] * low[i, t]
                left.append(col * inv[i])
            for i in range(8):
                reduced = reduced - left[i] * out[i]
            block[q] = reduced
        rows = out[0]
        for m in range(1, 8):
            rows = jnp.where(sub == m, out[m], rows)
        block[g] = rows
    return block


def factor_kernel(corner, work):
    work[...] = corner[...]
    sub = lax.broadcasted_iota(jnp.int32, (TILE, 128), 0)
    lane = lax.broadcasted_iota(jnp.int32, (TILE, 128), 1)
    right_eye = jnp.where(lane == sub + TILE, 1.0, 0.0)
    for k in range(TOP // TILE):
        o = TILE * k
        start = 128 * (o // 128)
        block = work[o : o + TILE, start : min(start + 128, TOP)]
        if start + 128 > TOP:
            block = jnp.concatenate([block, jnp.zeros((TILE, TILE), jnp.float32)], axis=1)
        if o != start:
            block = pltpu.roll(block, TILE, 1)
        block = jnp.where(lane < TILE, block, right_eye)
        groups = eliminate_block([block[8 * q : 8 * q + 8, :] for q in range(8)])
        block = jnp.concatenate(groups, axis=0)
        part = pltpu.roll(block, TILE, 1)[:, :TILE]
        row = lax.broadcasted_iota(jnp.int32, (TILE, TOP), 0)
        col = lax.broadcasted_iota(jnp.int32, (TILE, TOP), 1) - o
        own = (col >= 0) & (col < TILE)
        slab = dot(part, jnp.where(own, jnp.where(col == row, 1.0, 0.0), work[o : o + TILE, :]), ((1,), (0,)))
        work[o : o + TILE, :] = slab
        for top, bottom in ((o + TILE, o + 2 * TILE), (o + 2 * TILE, TOP)):
            if top >= TOP or top == bottom:
                continue
            update = dot(slab[:, top:bottom], slab, ((0,), (0,)))
            col = lax.broadcasted_iota(jnp.int32, (bottom - top, TOP), 1) - o
            own = (col >= 0) & (col < TILE)
            work[top:bottom, :] = jnp.where(own, 0.0, work[top:bottom, :]) - update


def factor_corner(corner):
    return pl.pallas_call(
        factor_kernel,
        out_shape=jax.ShapeDtypeStruct((TOP, TOP), jnp.float32),
        in_specs=[vmem()],
        out_specs=vmem(),
        compiler_params=pltpu.CompilerParams(vmem_limit_bytes=24 * MIB),
        cost_estimate=pl.CostEstimate(flops=25_000_000_000, bytes_accessed=2_700_000, transcendentals=1000),
        name="factor_corner",
    )(corner)


def weights_kernel(flags, side, corner, weights, solved):
    row = lax.broadcasted_iota(jnp.int32, (TOP, TOP), 0) // TILE
    col = lax.broadcasted_iota(jnp.int32, (TOP, TOP), 1) // TILE
    inverse = jnp.where(row >= col, corner[...], 0.0)
    solved[...] = dot(inverse, side[...], ((1,), (0,)))

    @pl.when(flags[2] == 0)
    def _():
        weights[...] = dot(inverse, solved[...], ((0,), (0,)))

    @pl.when(flags[2] == 1)
    def _():
        first = pl.multiple_of(flags[3] * PANEL, PANEL)
        row = (lax.broadcasted_iota(jnp.int32, (PANEL, TOP), 0) + first) // TILE
        col = lax.broadcasted_iota(jnp.int32, (PANEL, TOP), 1) // TILE
        own = jnp.where(row >= col, corner[pl.ds(first, PANEL), :], 0.0)
        row = lax.broadcasted_iota(jnp.int32, (TOP, TOP), 0)
        col = lax.broadcasted_iota(jnp.int32, (TOP, TOP), 1)
        weights[...] = -dot(jnp.where(row == col, 1.0, 0.0), own, ((1,), (1,)))


def make_weights(flags, side, corner):
    shape = jax.ShapeDtypeStruct((TOP, PANEL), jnp.float32)
    return pl.pallas_call(
        weights_kernel,
        out_shape=(shape, shape),
        in_specs=[smem(), vmem(), vmem()],
        out_specs=(vmem(), vmem()),
        compiler_params=pltpu.CompilerParams(vmem_limit_bytes=24 * MIB),
        cost_estimate=pl.CostEstimate(flops=3_000_000_000, bytes_accessed=2_500_000, transcendentals=0),
        name="make_weights",
    )(flags, side, corner)


def finish_kernel(flags, weights, side, corner, panel, base, out):
    lines = base.shape[1] // 128
    for pair in range(lines // 2):
        cols = []
        for line in (2 * pair, 2 * pair + 1):
            cols.append(jnp.concatenate([panel[t * lines + line] for t in range(9)], axis=0))
        update = dot(weights[...], jnp.concatenate(cols, axis=1), ((0,), (0,)))
        first = 256 * pair
        spot = slice(first, first + 256)
        col = lax.broadcasted_iota(jnp.int32, update.shape, 1) + first
        kept = jnp.where(flags[2] == 1, 0.0, base[:, spot])
        out[:, spot] = jnp.where(col < flags[0], 0.0, kept - update)

    @pl.when(flags[1] == 1)
    def _():
        row = lax.broadcasted_iota(jnp.int32, (TOP, TOP), 0) // PANEL
        col = lax.broadcasted_iota(jnp.int32, (TOP, TOP), 1) // PANEL
        strict = jnp.where(row < col, corner[...], 0.0)
        out[:, :TOP] = base[:, :TOP] - dot(side[...], strict, ((0,), (0,)))


def finish(flags, weights, side, corner, panel, base):
    return pl.pallas_call(
        finish_kernel,
        out_shape=jax.ShapeDtypeStruct(base.shape, jnp.float32),
        in_specs=[smem()] + [vmem()] * 5,
        out_specs=vmem(),
        compiler_params=pltpu.CompilerParams(vmem_limit_bytes=32 * MIB),
        cost_estimate=pl.CostEstimate(flops=2_500_000_000, bytes_accessed=9_000_000, transcendentals=0),
        name="finish",
    )(flags, weights, side, corner, panel, base)


def exchange(values, axes):
    return lax.all_to_all(values, axes, split_axis=0, concat_axis=0, tiled=True)


def local(front, child_tiles, child_target, child_rows, child_cols):
    my_row = lax.axis_index("row")
    my_sub = lax.axis_index("sub")
    my_col = lax.axis_index("col")
    my_block = my_sub * 8 + my_row
    block_rows, block_cols = front.shape
    order_tiles = FRONT // TILE
    tiles_down = block_rows // TILE
    tiles_across = block_cols // TILE
    here = tiles_down * tiles_across
    tile_row = child_target // order_tiles
    tile_col = child_target % order_tiles
    owner = tile_row // tiles_down
    place = (tile_row - owner * tiles_down) * tiles_across + tile_col - my_col * tiles_across
    slots, top_rows, slot_place = sort_tiles(
        owner, place, child_rows, child_cols, child_tiles.reshape(-1, HALF_ROWS, 128)
    )

    top_place = slot_place[:TOP_SLOTS]
    top_place = jnp.where(top_place < 0, -1, top_place + here * (jnp.arange(TOP_SLOTS) // CAP))
    meta = jnp.concatenate(
        [
            jnp.broadcast_to(top_place[None, :], (WIDE, TOP_SLOTS)),
            slot_place.reshape(WIDE, CAP),
            jnp.zeros((WIDE, 128 - TOP_SLOTS - CAP), jnp.int32),
        ],
        axis=1,
    ).astype(jnp.float32)
    front_rows = front.reshape(tiles_down, TILE, block_cols // 128, 128).transpose(1, 0, 2, 3)
    sent = jnp.concatenate(
        [top_rows.transpose(1, 0, 2), meta[:, None, :], front_rows.reshape(TILE, -1, 128)], axis=1
    )
    got = exchange(sent, ("sub", "row"))
    got_meta = got[:, STEPS, :].astype(jnp.int32)
    in_place = got_meta[:, TOP_SLOTS : TOP_SLOTS + CAP].reshape(-1)
    in_top = got_meta[:, :TOP_SLOTS].reshape(-1)
    pieces = got[:, :STEPS, :].reshape(-1, TILE)
    one_hot = (jnp.arange(STEPS * here, dtype=jnp.int32)[:, None] == in_top[None, :]).astype(jnp.float32)
    held = dot(one_hot, pieces, ((1,), (0,))).reshape(STEPS * tiles_down, block_cols)
    held = held + got[:STEPS, STEPS + 1 :, :].reshape(STEPS * tiles_down, block_cols)

    lines = block_cols // 128
    panel = lax.all_gather(held.reshape(9 * lines, 128), "row", axis=0, tiled=False).transpose(1, 0, 2)

    got = exchange(jnp.broadcast_to(held.reshape(1, 1, -1), (8, 1, held.size)), "col").reshape(8, 9, block_cols)
    got, panel = lax.optimization_barrier((got, panel))
    panel = lax.all_gather(panel, "sub", axis=1, tiled=True)
    side_size = 9 * PANEL
    side_send = got.reshape(8, 9, 8, PANEL).transpose(0, 2, 1, 3).reshape(WIDE, side_size)
    even = my_col % 2 == 0
    upper_half = got[0, 0:3, :TOP]
    lower_half = jnp.concatenate([got[0, 3:6, PANEL:TOP], got[0, 6:9, 2 * PANEL : TOP]], axis=1)
    corner_send = jnp.where(even, upper_half, lower_half).reshape(1, -1)
    corner_send = jnp.broadcast_to(corner_send, (WIDE, corner_send.size))
    got = exchange(jnp.concatenate([side_send, corner_send], axis=1), ("sub", "row"))
    got, slots = lax.optimization_barrier((got, slots))
    arrived = exchange(slots.reshape(WIDE, CAP * HALF_ROWS, 128), ("sub", "row")).reshape(SLOTS, HALF_ROWS, 128)
    side = got[:, :side_size].reshape(WIDE, 9, PANEL).transpose(1, 0, 2).reshape(TOP, PANEL)
    corner_mine = got[:, side_size:].reshape(WIDE, 3, TOP).transpose(1, 0, 2).reshape(PANEL, TOP)
    corner_other = lax.ppermute(corner_mine, "col", [(i, i ^ 1) for i in range(8)])
    first = jnp.where(even, corner_mine, corner_other)
    second = jnp.where(even, corner_other, corner_mine)

    def balanced(square):
        return 0.5 * (square + square.T)

    def blank(cols):
        return jnp.zeros((PANEL, cols), jnp.float32)

    corner = jnp.concatenate(
        [
            jnp.concatenate([balanced(first[:, :PANEL]), first[:, PANEL:]], axis=1),
            jnp.concatenate([blank(PANEL), balanced(second[:, :PANEL]), second[:, PANEL : 2 * PANEL]], axis=1),
            jnp.concatenate([blank(2 * PANEL), balanced(second[:, 2 * PANEL :])], axis=1),
        ],
        axis=0,
    )
    corner = factor_corner(corner)

    is_owner = my_block < STEPS
    flags = jnp.stack(
        [
            jnp.where(is_owner, my_block * PANEL - my_col * block_cols, 0),
            ((my_col == 0) & ~is_owner).astype(jnp.int32),
            is_owner.astype(jnp.int32),
            jnp.minimum(my_block, STEPS - 1),
        ]
    ).astype(jnp.int32)
    weights, solved_side = make_weights(flags, side, corner)
    matrix = extend(in_place, arrived, front)
    return finish(flags, weights, solved_side, corner, panel, matrix)


def solution(mesh):
    in_specs = (
        P(("sub", "row"), "col"),
        P(("sub", "row", "col"), None),
        P(("sub", "row", "col")),
        P(("sub", "row", "col")),
        P(("sub", "row", "col")),
    )
    out_specs = P(("sub", "row"), "col")
    return jax.shard_map(local, mesh=mesh, in_specs=in_specs, out_specs=out_specs, check_vma=False)
```

```python
import functools

import jax
import jax.numpy as jnp
from jax import lax
from jax.experimental import pallas as pl
from jax.experimental.pallas import tpu as pltpu
from jax.sharding import PartitionSpec as P

FRONT = 12288
TILE = 64
PANEL = 192
STEPS = 3
TOP = PANEL * STEPS
WIDE = 64
CAP = 2
SLOTS = WIDE * CAP
TOP_SLOTS = STEPS * CAP
HALF_ROWS = TILE // 2
HIGHEST = lax.Precision.HIGHEST
MIB = 1024 * 1024


def vmem():
    return pl.BlockSpec(memory_space=pltpu.VMEM)


def smem():
    return pl.BlockSpec(memory_space=pltpu.SMEM)


def dot(a, b, dims):
    return lax.dot_general(a, b, (dims, ((), ())), precision=HIGHEST, preferred_element_type=jnp.float32)


def split_halves(first, second):
    low = lax.broadcasted_iota(jnp.int32, first.shape, 1) < TILE
    even = jnp.where(low, first, pltpu.roll(second, TILE, 1))
    odd = jnp.where(low, pltpu.roll(first, TILE, 1), second)
    return even, odd


def sort_kernel(owner, place, rows, cols, tiles, slots, top_rows, slot_place, top_buf, count):
    def clear(i, _):
        count[i] = 0
        slot_place[2 * i] = -1
        slot_place[2 * i + 1] = -1
        return 0

    lax.fori_loop(0, WIDE, clear, 0)
    top_buf[...] = jnp.zeros_like(top_buf)
    line = lax.broadcasted_iota(jnp.int32, (HALF_ROWS, 128), 0)
    lane = lax.broadcasted_iota(jnp.int32, (HALF_ROWS, 128), 1)
    tile_row = 2 * line + lane // TILE
    tile_col = lane % TILE

    def one(k, _):
        to = owner[k]
        rank = jnp.minimum(count[to], CAP - 1)
        count[to] = rank + 1
        slot = CAP * to + rank
        slot_place[slot] = place[k]
        inside = (tile_row < rows[k]) & (tile_col < cols[k])
        kept = jnp.where(inside, tiles[k], 0.0)
        slots[slot] = kept

        @pl.when(to < STEPS)
        def _():
            top_buf[slot] = kept

        return 0

    lax.fori_loop(0, tiles.shape[0], one, 0)
    for q in range(STEPS):
        even, odd = split_halves(top_buf[2 * q], top_buf[2 * q + 1])
        top_rows[q, pl.ds(0, HALF_ROWS, stride=2), :] = even
        top_rows[q, pl.ds(1, HALF_ROWS, stride=2), :] = odd


def sort_tiles(owner, place, rows, cols, tiles):
    return pl.pallas_call(
        sort_kernel,
        out_shape=(
            jax.ShapeDtypeStruct((SLOTS, HALF_ROWS, 128), jnp.float32),
            jax.ShapeDtypeStruct((STEPS, TILE, 128), jnp.float32),
            jax.ShapeDtypeStruct((SLOTS,), jnp.int32),
        ),
        in_specs=[smem()] * 4 + [vmem()],
        out_specs=(vmem(), vmem(), smem()),
        scratch_shapes=[
            pltpu.VMEM((TOP_SLOTS, HALF_ROWS, 128), jnp.float32),
            pltpu.SMEM((WIDE,), jnp.int32),
        ],
        compiler_params=pltpu.CompilerParams(vmem_limit_bytes=24 * MIB),
        cost_estimate=pl.CostEstimate(flops=1_000_000, bytes_accessed=3_200_000, transcendentals=0),
        name="sort_tiles",
    )(owner, place, rows, cols, tiles)


def extend_kernel(place, tiles, front, out, total, stage):
    down, across = front.shape[0] // TILE, front.shape[1] // TILE
    total[...] = jnp.zeros_like(total)

    def one(n, _):
        at = place[n]
        at = jnp.where(at < 0, down * across, at)
        total[at] = total[at] + tiles[n]
        return 0

    lax.fori_loop(0, tiles.shape[0], one, 0)
    for r in range(down):
        for pair in range(across // 2):
            at = r * across + 2 * pair
            even, odd = split_halves(total[at], total[at + 1])
            stage[at // 2, pl.ds(0, HALF_ROWS, stride=2), :] = even
            stage[at // 2, pl.ds(1, HALF_ROWS, stride=2), :] = odd
            spot = (slice(TILE * r, TILE * r + TILE), slice(128 * pair, 128 * pair + 128))
            out[spot] = front[spot] + stage[at // 2]


def extend(place, tiles, front):
    count = (front.shape[0] // TILE) * (front.shape[1] // TILE)
    return pl.pallas_call(
        extend_kernel,
        out_shape=jax.ShapeDtypeStruct(front.shape, jnp.float32),
        in_specs=[smem(), vmem(), vmem()],
        out_specs=vmem(),
        scratch_shapes=[
            pltpu.VMEM((count + 1, HALF_ROWS, 128), jnp.float32),
            pltpu.VMEM((count // 2, TILE, 128), jnp.float32),
        ],
        compiler_params=pltpu.CompilerParams(vmem_limit_bytes=24 * MIB),
        cost_estimate=pl.CostEstimate(flops=1_000_000, bytes_accessed=4_500_000, transcendentals=0),
        name="extend",
    )(place, tiles, front)


def lanes_of(group, col):
    return jnp.broadcast_to(group[:, col : col + 1], (8, 128))


def row_of(group, row):
    return jnp.broadcast_to(group[row : row + 1, :], (8, 128))


def eliminate_block(block):
    sub = lax.broadcasted_iota(jnp.int32, (8, 128), 0)
    for g in range(8):
        spread = [lanes_of(block[g], 8 * g + i) for i in range(8)]
        pivot = {(m, n): row_of(spread[n], m) for m in range(8) for n in range(m, 8)}
        low = {}
        inv = [None] * 8
        for i in range(0, 8, 2):
            a, b, c = pivot[i, i], pivot[i, i + 1], pivot[i + 1, i + 1]
            inv[i] = lax.rsqrt(a)
            inv[i + 1] = (a * inv[i]) * lax.rsqrt(a * c - b * b)
            low[i + 1, i] = b * inv[i]
            for m in range(i + 2, 8):
                low[m, i] = pivot[i, m] * inv[i]
                low[m, i + 1] = (pivot[i + 1, m] - low[m, i] * low[i + 1, i]) * inv[i + 1]
            for m in range(i + 2, 8):
                for n in range(m, 8):
                    pivot[m, n] = pivot[m, n] - low[m, i] * low[n, i] - low[m, i + 1] * low[n, i + 1]
        out = []
        for m in range(8):
            row = row_of(block[g], m)
            for t in range(m):
                row = row - low[m, t] * out[t]
            out.append(row * inv[m])
        for q in range(g + 1, 8):
            left = []
            reduced = block[q]
            for i in range(8):
                col = lanes_of(block[q], 8 * g + i)
                for t in range(i):
                    col = col - left[t] * low[i, t]
                left.append(col * inv[i])
            for i in range(8):
                reduced = reduced - left[i] * out[i]
            block[q] = reduced
        rows = out[0]
        for m in range(1, 8):
            rows = jnp.where(sub == m, out[m], rows)
        block[g] = rows
    return block


def factor_kernel(corner, work):
    work[...] = corner[...]
    sub = lax.broadcasted_iota(jnp.int32, (TILE, 128), 0)
    lane = lax.broadcasted_iota(jnp.int32, (TILE, 128), 1)
    right_eye = jnp.where(lane == sub + TILE, 1.0, 0.0)
    for k in range(TOP // TILE):
        o = TILE * k
        start = 128 * (o // 128)
        block = work[o : o + TILE, start : min(start + 128, TOP)]
        if start + 128 > TOP:
            block = jnp.concatenate([block, jnp.zeros((TILE, TILE), jnp.float32)], axis=1)
        if o != start:
            block = pltpu.roll(block, TILE, 1)
        block = jnp.where(lane < TILE, block, right_eye)
        groups = eliminate_block([block[8 * q : 8 * q + 8, :] for q in range(8)])
        block = jnp.concatenate(groups, axis=0)
        part = pltpu.roll(block, TILE, 1)[:, :TILE]
        row = lax.broadcasted_iota(jnp.int32, (TILE, TOP), 0)
        col = lax.broadcasted_iota(jnp.int32, (TILE, TOP), 1) - o
        own = (col >= 0) & (col < TILE)
        slab = dot(part, jnp.where(own, jnp.where(col == row, 1.0, 0.0), work[o : o + TILE, :]), ((1,), (0,)))
        work[o : o + TILE, :] = slab
        for top, bottom in ((o + TILE, o + 2 * TILE), (o + 2 * TILE, TOP)):
            if top >= TOP or top == bottom:
                continue
            update = dot(slab[:, top:bottom], slab, ((0,), (0,)))
            col = lax.broadcasted_iota(jnp.int32, (bottom - top, TOP), 1) - o
            own = (col >= 0) & (col < TILE)
            work[top:bottom, :] = jnp.where(own, 0.0, work[top:bottom, :]) - update


def factor_corner(corner):
    return pl.pallas_call(
        factor_kernel,
        out_shape=jax.ShapeDtypeStruct((TOP, TOP), jnp.float32),
        in_specs=[vmem()],
        out_specs=vmem(),
        compiler_params=pltpu.CompilerParams(vmem_limit_bytes=24 * MIB),
        cost_estimate=pl.CostEstimate(flops=25_000_000_000, bytes_accessed=2_700_000, transcendentals=1000),
        name="factor_corner",
    )(corner)


def weights_kernel(flags, side, corner, weights, solved):
    row = lax.broadcasted_iota(jnp.int32, (TOP, TOP), 0) // TILE
    col = lax.broadcasted_iota(jnp.int32, (TOP, TOP), 1) // TILE
    inverse = jnp.where(row >= col, corner[...], 0.0)
    solved[...] = dot(inverse, side[...], ((1,), (0,)))

    @pl.when(flags[2] == 0)
    def _():
        weights[...] = dot(inverse, solved[...], ((0,), (0,)))

    @pl.when(flags[2] == 1)
    def _():
        first = pl.multiple_of(flags[3] * PANEL, PANEL)
        row = (lax.broadcasted_iota(jnp.int32, (PANEL, TOP), 0) + first) // TILE
        col = lax.broadcasted_iota(jnp.int32, (PANEL, TOP), 1) // TILE
        own = jnp.where(row >= col, corner[pl.ds(first, PANEL), :], 0.0)
        row = lax.broadcasted_iota(jnp.int32, (TOP, TOP), 0)
        col = lax.broadcasted_iota(jnp.int32, (TOP, TOP), 1)
        weights[...] = -dot(jnp.where(row == col, 1.0, 0.0), own, ((1,), (1,)))


def make_weights(flags, side, corner):
    shape = jax.ShapeDtypeStruct((TOP, PANEL), jnp.float32)
    return pl.pallas_call(
        weights_kernel,
        out_shape=(shape, shape),
        in_specs=[smem(), vmem(), vmem()],
        out_specs=(vmem(), vmem()),
        compiler_params=pltpu.CompilerParams(vmem_limit_bytes=24 * MIB),
        cost_estimate=pl.CostEstimate(flops=3_000_000_000, bytes_accessed=2_500_000, transcendentals=0),
        name="make_weights",
    )(flags, side, corner)


def finish_kernel(flags, weights, side, corner, panel, base, out):
    lines = base.shape[1] // 128
    for pair in range(lines // 2):
        cols = []
        for line in (2 * pair, 2 * pair + 1):
            cols.append(jnp.concatenate([panel[t * lines + line] for t in range(9)], axis=0))
        update = dot(weights[...], jnp.concatenate(cols, axis=1), ((0,), (0,)))
        first = 256 * pair
        spot = slice(first, first + 256)
        col = lax.broadcasted_iota(jnp.int32, update.shape, 1) + first
        kept = jnp.where(flags[2] == 1, 0.0, base[:, spot])
        out[:, spot] = jnp.where(col < flags[0], 0.0, kept - update)

    @pl.when(flags[1] == 1)
    def _():
        row = lax.broadcasted_iota(jnp.int32, (TOP, TOP), 0) // PANEL
        col = lax.broadcasted_iota(jnp.int32, (TOP, TOP), 1) // PANEL
        strict = jnp.where(row < col, corner[...], 0.0)
        out[:, :TOP] = base[:, :TOP] - dot(side[...], strict, ((0,), (0,)))


def finish(flags, weights, side, corner, panel, base):
    return pl.pallas_call(
        finish_kernel,
        out_shape=jax.ShapeDtypeStruct(base.shape, jnp.float32),
        in_specs=[smem()] + [vmem()] * 5,
        out_specs=vmem(),
        compiler_params=pltpu.CompilerParams(vmem_limit_bytes=32 * MIB),
        cost_estimate=pl.CostEstimate(flops=2_500_000_000, bytes_accessed=9_000_000, transcendentals=0),
        name="finish",
    )(flags, weights, side, corner, panel, base)


def exchange(values, axes):
    return lax.all_to_all(values, axes, split_axis=0, concat_axis=0, tiled=True)


def local(front, child_tiles, child_target, child_rows, child_cols):
    my_row = lax.axis_index("row")
    my_sub = lax.axis_index("sub")
    my_col = lax.axis_index("col")
    my_block = my_sub * 8 + my_row
    block_rows, block_cols = front.shape
    order_tiles = FRONT // TILE
    tiles_down = block_rows // TILE
    tiles_across = block_cols // TILE
    here = tiles_down * tiles_across
    tile_row = child_target // order_tiles
    tile_col = child_target % order_tiles
    owner = tile_row // tiles_down
    place = (tile_row - owner * tiles_down) * tiles_across + tile_col - my_col * tiles_across
    slots, top_rows, slot_place = sort_tiles(
        owner, place, child_rows, child_cols, child_tiles.reshape(-1, HALF_ROWS, 128)
    )

    top_place = slot_place[:TOP_SLOTS]
    top_place = jnp.where(top_place < 0, -1, top_place + here * (jnp.arange(TOP_SLOTS) // CAP))
    meta = jnp.concatenate(
        [
            jnp.broadcast_to(top_place[None, :], (WIDE, TOP_SLOTS)),
            slot_place.reshape(WIDE, CAP),
            jnp.zeros((WIDE, 128 - TOP_SLOTS - CAP), jnp.int32),
        ],
        axis=1,
    ).astype(jnp.float32)
    front_rows = front.reshape(tiles_down, TILE, block_cols // 128, 128).transpose(1, 0, 2, 3)
    sent = jnp.concatenate(
        [top_rows.transpose(1, 0, 2), meta[:, None, :], front_rows.reshape(TILE, -1, 128)], axis=1
    )
    got = exchange(sent, ("sub", "row"))
    got_meta = got[:, STEPS, :].astype(jnp.int32)
    in_place = got_meta[:, TOP_SLOTS : TOP_SLOTS + CAP].reshape(-1)
    in_top = got_meta[:, :TOP_SLOTS].reshape(-1)
    pieces = got[:, :STEPS, :].reshape(-1, TILE)
    one_hot = (jnp.arange(STEPS * here, dtype=jnp.int32)[:, None] == in_top[None, :]).astype(jnp.float32)
    held = dot(one_hot, pieces, ((1,), (0,))).reshape(STEPS * tiles_down, block_cols)
    held = held + got[:STEPS, STEPS + 1 :, :].reshape(STEPS * tiles_down, block_cols)

    lines = block_cols // 128
    piece = held.reshape(1, 9 * lines, 128)
    panel = exchange(jnp.broadcast_to(piece, (8,) + piece.shape[1:]), "row").transpose(1, 0, 2)
    held, panel = lax.optimization_barrier((held, panel))
    panel = lax.all_gather(panel, "sub", axis=1, tiled=True)

    got = exchange(jnp.broadcast_to(held.reshape(1, 1, -1), (8, 1, held.size)), "col").reshape(8, 9, block_cols)
    side_size = 9 * PANEL
    side_send = got.reshape(8, 9, 8, PANEL).transpose(0, 2, 1, 3).reshape(WIDE, side_size)
    even = my_col % 2 == 0
    upper_half = got[0, 0:3, :TOP]
    lower_half = jnp.concatenate([got[0, 3:6, PANEL:TOP], got[0, 6:9, 2 * PANEL : TOP]], axis=1)
    corner_send = jnp.where(even, upper_half, lower_half).reshape(1, -1)
    corner_send = jnp.broadcast_to(corner_send, (WIDE, corner_send.size))
    got = exchange(jnp.concatenate([side_send, corner_send], axis=1), ("sub", "row"))
    got, slots = lax.optimization_barrier((got, slots))
    arrived = exchange(slots.reshape(WIDE, CAP * HALF_ROWS, 128), ("sub", "row")).reshape(SLOTS, HALF_ROWS, 128)
    side = got[:, :side_size].reshape(WIDE, 9, PANEL).transpose(1, 0, 2).reshape(TOP, PANEL)
    corner_mine = got[:, side_size:].reshape(WIDE, 3, TOP).transpose(1, 0, 2).reshape(PANEL, TOP)
    corner_other = lax.ppermute(corner_mine, "col", [(i, i ^ 1) for i in range(8)])
    first = jnp.where(even, corner_mine, corner_other)
    second = jnp.where(even, corner_other, corner_mine)

    def balanced(square):
        return 0.5 * (square + square.T)

    def blank(cols):
        return jnp.zeros((PANEL, cols), jnp.float32)

    corner = jnp.concatenate(
        [
            jnp.concatenate([balanced(first[:, :PANEL]), first[:, PANEL:]], axis=1),
            jnp.concatenate([blank(PANEL), balanced(second[:, :PANEL]), second[:, PANEL : 2 * PANEL]], axis=1),
            jnp.concatenate([blank(2 * PANEL), balanced(second[:, 2 * PANEL :])], axis=1),
        ],
        axis=0,
    )
    corner = factor_corner(corner)

    is_owner = my_block < STEPS
    flags = jnp.stack(
        [
            jnp.where(is_owner, my_block * PANEL - my_col * block_cols, 0),
            ((my_col == 0) & ~is_owner).astype(jnp.int32),
            is_owner.astype(jnp.int32),
            jnp.minimum(my_block, STEPS - 1),
        ]
    ).astype(jnp.int32)
    weights, solved_side = make_weights(flags, side, corner)
    matrix = extend(in_place, arrived, front)
    return finish(flags, weights, solved_side, corner, panel, matrix)


def solution(mesh):
    in_specs = (
        P(("sub", "row"), "col"),
        P(("sub", "row", "col"), None),
        P(("sub", "row", "col")),
        P(("sub", "row", "col")),
        P(("sub", "row", "col")),
    )
    out_specs = P(("sub", "row"), "col")
    return jax.shard_map(local, mesh=mesh, in_specs=in_specs, out_specs=out_specs, check_vma=False)
```

```python
import functools

import jax
import jax.numpy as jnp
from jax import lax
from jax.experimental import pallas as pl
from jax.experimental.pallas import tpu as pltpu
from jax.sharding import PartitionSpec as P

FRONT = 12288
TILE = 64
PANEL = 192
STEPS = 3
TOP = PANEL * STEPS
WIDE = 64
CAP = 2
SLOTS = WIDE * CAP
TOP_SLOTS = STEPS * CAP
HALF_ROWS = TILE // 2
HIGHEST = lax.Precision.HIGHEST
MIB = 1024 * 1024


def vmem():
    return pl.BlockSpec(memory_space=pltpu.VMEM)


def smem():
    return pl.BlockSpec(memory_space=pltpu.SMEM)


def dot(a, b, dims):
    return lax.dot_general(a, b, (dims, ((), ())), precision=HIGHEST, preferred_element_type=jnp.float32)


def split_halves(first, second):
    low = lax.broadcasted_iota(jnp.int32, first.shape, 1) < TILE
    even = jnp.where(low, first, pltpu.roll(second, TILE, 1))
    odd = jnp.where(low, pltpu.roll(first, TILE, 1), second)
    return even, odd


def sort_kernel(owner, place, rows, cols, tiles, slots, top_rows, slot_place, top_buf, count):
    def clear(i, _):
        count[i] = 0
        slot_place[2 * i] = -1
        slot_place[2 * i + 1] = -1
        return 0

    lax.fori_loop(0, WIDE, clear, 0)
    top_buf[...] = jnp.zeros_like(top_buf)
    line = lax.broadcasted_iota(jnp.int32, (HALF_ROWS, 128), 0)
    lane = lax.broadcasted_iota(jnp.int32, (HALF_ROWS, 128), 1)
    tile_row = 2 * line + lane // TILE
    tile_col = lane % TILE

    def one(k, _):
        to = owner[k]
        rank = jnp.minimum(count[to], CAP - 1)
        count[to] = rank + 1
        slot = CAP * to + rank
        slot_place[slot] = place[k]
        inside = (tile_row < rows[k]) & (tile_col < cols[k])
        kept = jnp.where(inside, tiles[k], 0.0)
        slots[slot] = kept

        @pl.when(to < STEPS)
        def _():
            top_buf[slot] = kept

        return 0

    lax.fori_loop(0, tiles.shape[0], one, 0)
    for q in range(STEPS):
        even, odd = split_halves(top_buf[2 * q], top_buf[2 * q + 1])
        top_rows[q, pl.ds(0, HALF_ROWS, stride=2), :] = even
        top_rows[q, pl.ds(1, HALF_ROWS, stride=2), :] = odd


def sort_tiles(owner, place, rows, cols, tiles):
    return pl.pallas_call(
        sort_kernel,
        out_shape=(
            jax.ShapeDtypeStruct((SLOTS, HALF_ROWS, 128), jnp.float32),
            jax.ShapeDtypeStruct((STEPS, TILE, 128), jnp.float32),
            jax.ShapeDtypeStruct((SLOTS,), jnp.int32),
        ),
        in_specs=[smem()] * 4 + [vmem()],
        out_specs=(vmem(), vmem(), smem()),
        scratch_shapes=[
            pltpu.VMEM((TOP_SLOTS, HALF_ROWS, 128), jnp.float32),
            pltpu.SMEM((WIDE,), jnp.int32),
        ],
        compiler_params=pltpu.CompilerParams(vmem_limit_bytes=24 * MIB),
        cost_estimate=pl.CostEstimate(flops=1_000_000, bytes_accessed=3_200_000, transcendentals=0),
        name="sort_tiles",
    )(owner, place, rows, cols, tiles)


def extend_kernel(place, tiles, front, out, total, stage):
    down, across = front.shape[0] // TILE, front.shape[1] // TILE
    total[...] = jnp.zeros_like(total)

    def one(n, _):
        at = place[n]
        at = jnp.where(at < 0, down * across, at)
        total[at] = total[at] + tiles[n]
        return 0

    lax.fori_loop(0, tiles.shape[0], one, 0)
    for r in range(down):
        for pair in range(across // 2):
            at = r * across + 2 * pair
            even, odd = split_halves(total[at], total[at + 1])
            stage[at // 2, pl.ds(0, HALF_ROWS, stride=2), :] = even
            stage[at // 2, pl.ds(1, HALF_ROWS, stride=2), :] = odd
            spot = (slice(TILE * r, TILE * r + TILE), slice(128 * pair, 128 * pair + 128))
            out[spot] = front[spot] + stage[at // 2]


def extend(place, tiles, front):
    count = (front.shape[0] // TILE) * (front.shape[1] // TILE)
    return pl.pallas_call(
        extend_kernel,
        out_shape=jax.ShapeDtypeStruct(front.shape, jnp.float32),
        in_specs=[smem(), vmem(), vmem()],
        out_specs=vmem(),
        scratch_shapes=[
            pltpu.VMEM((count + 1, HALF_ROWS, 128), jnp.float32),
            pltpu.VMEM((count // 2, TILE, 128), jnp.float32),
        ],
        compiler_params=pltpu.CompilerParams(vmem_limit_bytes=24 * MIB),
        cost_estimate=pl.CostEstimate(flops=1_000_000, bytes_accessed=4_500_000, transcendentals=0),
        name="extend",
    )(place, tiles, front)


def lanes_of(group, col):
    return jnp.broadcast_to(group[:, col : col + 1], (8, 128))


def row_of(group, row):
    return jnp.broadcast_to(group[row : row + 1, :], (8, 128))


def eliminate_block(block):
    sub = lax.broadcasted_iota(jnp.int32, (8, 128), 0)
    for g in range(8):
        spread = [lanes_of(block[g], 8 * g + i) for i in range(8)]
        pivot = {(m, n): row_of(spread[n], m) for m in range(8) for n in range(m, 8)}
        low = {}
        inv = [None] * 8
        for i in range(0, 8, 2):
            a, b, c = pivot[i, i], pivot[i, i + 1], pivot[i + 1, i + 1]
            inv[i] = lax.rsqrt(a)
            inv[i + 1] = (a * inv[i]) * lax.rsqrt(a * c - b * b)
            low[i + 1, i] = b * inv[i]
            for m in range(i + 2, 8):
                low[m, i] = pivot[i, m] * inv[i]
                low[m, i + 1] = (pivot[i + 1, m] - low[m, i] * low[i + 1, i]) * inv[i + 1]
            for m in range(i + 2, 8):
                for n in range(m, 8):
                    pivot[m, n] = pivot[m, n] - low[m, i] * low[n, i] - low[m, i + 1] * low[n, i + 1]
        out = []
        for m in range(8):
            row = row_of(block[g], m)
            for t in range(m):
                row = row - low[m, t] * out[t]
            out.append(row * inv[m])
        for q in range(g + 1, 8):
            left = []
            reduced = block[q]
            for i in range(8):
                col = lanes_of(block[q], 8 * g + i)
                for t in range(i):
                    col = col - left[t] * low[i, t]
                left.append(col * inv[i])
            for i in range(8):
                reduced = reduced - left[i] * out[i]
            block[q] = reduced
        rows = out[0]
        for m in range(1, 8):
            rows = jnp.where(sub == m, out[m], rows)
        block[g] = rows
    return block


def factor_kernel(corner, work):
    work[...] = corner[...]
    sub = lax.broadcasted_iota(jnp.int32, (TILE, 128), 0)
    lane = lax.broadcasted_iota(jnp.int32, (TILE, 128), 1)
    right_eye = jnp.where(lane == sub + TILE, 1.0, 0.0)
    for k in range(TOP // TILE):
        o = TILE * k
        start = 128 * (o // 128)
        block = work[o : o + TILE, start : min(start + 128, TOP)]
        if start + 128 > TOP:
            block = jnp.concatenate([block, jnp.zeros((TILE, TILE), jnp.float32)], axis=1)
        if o != start:
            block = pltpu.roll(block, TILE, 1)
        block = jnp.where(lane < TILE, block, right_eye)
        groups = eliminate_block([block[8 * q : 8 * q + 8, :] for q in range(8)])
        block = jnp.concatenate(groups, axis=0)
        part = pltpu.roll(block, TILE, 1)[:, :TILE]
        row = lax.broadcasted_iota(jnp.int32, (TILE, TOP), 0)
        col = lax.broadcasted_iota(jnp.int32, (TILE, TOP), 1) - o
        own = (col >= 0) & (col < TILE)
        slab = dot(part, jnp.where(own, jnp.where(col == row, 1.0, 0.0), work[o : o + TILE, :]), ((1,), (0,)))
        work[o : o + TILE, :] = slab
        for top, bottom in ((o + TILE, o + 2 * TILE), (o + 2 * TILE, TOP)):
            if top >= TOP or top == bottom:
                continue
            update = dot(slab[:, top:bottom], slab, ((0,), (0,)))
            col = lax.broadcasted_iota(jnp.int32, (bottom - top, TOP), 1) - o
            own = (col >= 0) & (col < TILE)
            work[top:bottom, :] = jnp.where(own, 0.0, work[top:bottom, :]) - update


def factor_corner(corner):
    return pl.pallas_call(
        factor_kernel,
        out_shape=jax.ShapeDtypeStruct((TOP, TOP), jnp.float32),
        in_specs=[vmem()],
        out_specs=vmem(),
        compiler_params=pltpu.CompilerParams(vmem_limit_bytes=24 * MIB),
        cost_estimate=pl.CostEstimate(flops=25_000_000_000, bytes_accessed=2_700_000, transcendentals=1000),
        name="factor_corner",
    )(corner)


def panel_order():
    row = lax.broadcasted_iota(jnp.int32, (TOP, TOP), 0)
    col = lax.broadcasted_iota(jnp.int32, (TOP, TOP), 1)
    source = jnp.where(row < 8 * WIDE, (row % 8) * WIDE + row // 8, row)
    return jnp.where(col == source, 1.0, 0.0)


def weights_kernel(flags, side, corner, weights, solved):
    row = lax.broadcasted_iota(jnp.int32, (TOP, TOP), 0) // TILE
    col = lax.broadcasted_iota(jnp.int32, (TOP, TOP), 1) // TILE
    inverse = jnp.where(row >= col, corner[...], 0.0)
    solved[...] = dot(inverse, side[...], ((1,), (0,)))
    order = panel_order()

    @pl.when(flags[2] == 0)
    def _():
        weights[...] = dot(order, dot(inverse, solved[...], ((0,), (0,))), ((1,), (0,)))

    @pl.when(flags[2] == 1)
    def _():
        first = pl.multiple_of(flags[3] * PANEL, PANEL)
        row = (lax.broadcasted_iota(jnp.int32, (PANEL, TOP), 0) + first) // TILE
        col = lax.broadcasted_iota(jnp.int32, (PANEL, TOP), 1) // TILE
        own = jnp.where(row >= col, corner[pl.ds(first, PANEL), :], 0.0)
        weights[...] = -dot(order, own, ((1,), (1,)))


def make_weights(flags, side, corner):
    shape = jax.ShapeDtypeStruct((TOP, PANEL), jnp.float32)
    return pl.pallas_call(
        weights_kernel,
        out_shape=(shape, shape),
        in_specs=[smem(), vmem(), vmem()],
        out_specs=(vmem(), vmem()),
        compiler_params=pltpu.CompilerParams(vmem_limit_bytes=24 * MIB),
        cost_estimate=pl.CostEstimate(flops=3_000_000_000, bytes_accessed=2_500_000, transcendentals=0),
        name="make_weights",
    )(flags, side, corner)


def finish_kernel(flags, weights, side, corner, panel, base, out):
    lines = base.shape[1] // 128
    for pair in range(lines // 2):
        cols = []
        for line in (2 * pair, 2 * pair + 1):
            block = panel[:, 8 * line : 8 * line + 8, :].reshape(8 * WIDE, 128)
            last = panel[:, 8 * lines + line, :]
            cols.append(jnp.concatenate([block, last], axis=0))
        update = dot(weights[...], jnp.concatenate(cols, axis=1), ((0,), (0,)))
        first = 256 * pair
        spot = slice(first, first + 256)
        col = lax.broadcasted_iota(jnp.int32, update.shape, 1) + first
        kept = jnp.where(flags[2] == 1, 0.0, base[:, spot])
        out[:, spot] = jnp.where(col < flags[0], 0.0, kept - update)

    @pl.when(flags[1] == 1)
    def _():
        row = lax.broadcasted_iota(jnp.int32, (TOP, TOP), 0) // PANEL
        col = lax.broadcasted_iota(jnp.int32, (TOP, TOP), 1) // PANEL
        strict = jnp.where(row < col, corner[...], 0.0)
        out[:, :TOP] = base[:, :TOP] - dot(side[...], strict, ((0,), (0,)))


def finish(flags, weights, side, corner, panel, base):
    return pl.pallas_call(
        finish_kernel,
        out_shape=jax.ShapeDtypeStruct(base.shape, jnp.float32),
        in_specs=[smem()] + [vmem()] * 5,
        out_specs=vmem(),
        compiler_params=pltpu.CompilerParams(vmem_limit_bytes=56 * MIB),
        cost_estimate=pl.CostEstimate(flops=2_500_000_000, bytes_accessed=9_000_000, transcendentals=0),
        name="finish",
    )(flags, weights, side, corner, panel, base)


def exchange(values, axes):
    return lax.all_to_all(values, axes, split_axis=0, concat_axis=0, tiled=True)


def local(front, child_tiles, child_target, child_rows, child_cols):
    my_row = lax.axis_index("row")
    my_sub = lax.axis_index("sub")
    my_col = lax.axis_index("col")
    my_block = my_sub * 8 + my_row
    block_rows, block_cols = front.shape
    order_tiles = FRONT // TILE
    tiles_down = block_rows // TILE
    tiles_across = block_cols // TILE
    here = tiles_down * tiles_across
    tile_row = child_target // order_tiles
    tile_col = child_target % order_tiles
    owner = tile_row // tiles_down
    place = (tile_row - owner * tiles_down) * tiles_across + tile_col - my_col * tiles_across
    slots, top_rows, slot_place = sort_tiles(
        owner, place, child_rows, child_cols, child_tiles.reshape(-1, HALF_ROWS, 128)
    )

    top_place = slot_place[:TOP_SLOTS]
    top_place = jnp.where(top_place < 0, -1, top_place + here * (jnp.arange(TOP_SLOTS) // CAP))
    meta = jnp.concatenate(
        [
            jnp.broadcast_to(top_place[None, :], (WIDE, TOP_SLOTS)),
            slot_place.reshape(WIDE, CAP),
            jnp.zeros((WIDE, 128 - TOP_SLOTS - CAP), jnp.int32),
        ],
        axis=1,
    ).astype(jnp.float32)
    front_rows = front.reshape(tiles_down, TILE, block_cols // 128, 128).transpose(1, 0, 2, 3)
    sent = jnp.concatenate(
        [top_rows.transpose(1, 0, 2), meta[:, None, :], front_rows.reshape(TILE, -1, 128)], axis=1
    )
    got = exchange(sent, ("sub", "row"))
    got_meta = got[:, STEPS, :].astype(jnp.int32)
    in_place = got_meta[:, TOP_SLOTS : TOP_SLOTS + CAP].reshape(-1)
    in_top = got_meta[:, :TOP_SLOTS].reshape(-1)
    pieces = got[:, :STEPS, :].reshape(-1, TILE)
    one_hot = (jnp.arange(STEPS * here, dtype=jnp.int32)[:, None] == in_top[None, :]).astype(jnp.float32)
    held = dot(one_hot, pieces, ((1,), (0,))).reshape(STEPS * tiles_down, block_cols)
    held = held + got[:STEPS, STEPS + 1 :, :].reshape(STEPS * tiles_down, block_cols)

    lines = block_cols // 128
    whole = held[:8].reshape(8, lines, 128).transpose(1, 0, 2).reshape(8 * lines, 128)
    panel = lax.all_gather(
        jnp.concatenate([whole, held[8].reshape(lines, 128)], axis=0), ("sub", "row"), axis=0, tiled=False
    )

    part_cols = PANEL // 8
    side_size = 9 * part_cols
    packed = jnp.concatenate([held[0:3, :TOP], held[3:6, PANEL:TOP], held[6:9, 2 * PANEL : TOP]], axis=1)
    corner_cols = packed.shape[1] // 8
    corner_send = packed.reshape(3, 8, corner_cols).transpose(1, 0, 2).reshape(8, -1)
    side_send = held.reshape(9, 8, 8, part_cols).transpose(2, 1, 0, 3).reshape(8, -1)
    got = exchange(jnp.concatenate([side_send, corner_send], axis=1), "col")
    side_send = got[:, : 8 * side_size].reshape(WIDE, side_size)
    corner_send = jnp.broadcast_to(got[0:1, 8 * side_size :], (WIDE, 3 * corner_cols))
    got = exchange(jnp.concatenate([side_send, corner_send], axis=1), ("sub", "row"))
    got, slots = lax.optimization_barrier((got, slots))
    arrived = exchange(slots.reshape(WIDE, CAP * HALF_ROWS, 128), ("sub", "row")).reshape(SLOTS, HALF_ROWS, 128)
    got = exchange(jnp.broadcast_to(got[None], (8,) + got.shape), "col")
    side = got[:, :, :side_size].reshape(8, WIDE, 9, part_cols).transpose(2, 1, 0, 3).reshape(TOP, PANEL)
    packed = got[:, :, side_size:].reshape(8, WIDE, 3, corner_cols).transpose(2, 1, 0, 3).reshape(PANEL, -1)

    def balanced(square):
        return 0.5 * (square + square.T)

    def blank(cols):
        return jnp.zeros((PANEL, cols), jnp.float32)

    second = packed[:, TOP : TOP + 2 * PANEL]
    corner = jnp.concatenate(
        [
            jnp.concatenate([balanced(packed[:, :PANEL]), packed[:, PANEL:TOP]], axis=1),
            jnp.concatenate([blank(PANEL), balanced(second[:, :PANEL]), second[:, PANEL:]], axis=1),
            jnp.concatenate([blank(2 * PANEL), balanced(packed[:, TOP + 2 * PANEL :])], axis=1),
        ],
        axis=0,
    )
    corner = factor_corner(corner)

    is_owner = my_block < STEPS
    flags = jnp.stack(
        [
            jnp.where(is_owner, my_block * PANEL - my_col * block_cols, 0),
            ((my_col == 0) & ~is_owner).astype(jnp.int32),
            is_owner.astype(jnp.int32),
            jnp.minimum(my_block, STEPS - 1),
        ]
    ).astype(jnp.int32)
    weights, solved_side = make_weights(flags, side, corner)
    matrix = extend(in_place, arrived, front)
    return finish(flags, weights, solved_side, corner, panel, matrix)


def solution(mesh):
    in_specs = (
        P(("sub", "row"), "col"),
        P(("sub", "row", "col"), None),
        P(("sub", "row", "col")),
        P(("sub", "row", "col")),
        P(("sub", "row", "col")),
    )
    out_specs = P(("sub", "row"), "col")
    return jax.shard_map(local, mesh=mesh, in_specs=in_specs, out_specs=out_specs, check_vma=False)
```
